32 devices in a mesh: seq: 16 (over z, x, core), mp: 2 (over y).
Axes of the slice: x: 2, y: 2, z: 4, core: 2. Of those that a mesh axis runs over, the one named last changes fastest.
Arguments:
- q_new: bfloat16 [4096, 3072], P('seq', 'mp'), may hold values from -100 to 100
- k_new: bfloat16 [4096, 3072], P('seq', 'mp'), may hold values from -100 to 100
- v_new: bfloat16 [4096, 3072], P('seq', 'mp'), may hold values from -6 to 6
- q_gain: float32 [3072], P('mp'), may hold values from 0.1 to 1.9
- k_gain: float32 [3072], P('mp'), may hold values from 0.1 to 1.9
- cache_k: bfloat16 [256, 128, 3072], P('seq', None, 'mp'), may hold values from -300 to 300
- cache_v: bfloat16 [256, 128, 3072], P('seq', None, 'mp'), may hold values from -6 to 6
- new_count: int32 [16, 2], replicated, may hold values from 1 to 192, 256 in all within a row
- prefix_blocks: int32 [32], replicated, may hold values from 0 to 16, as said below
- block_req: int32 [256], replicated, may hold values from 0 to 31, as said below
Outputs:
- attended: bfloat16 [4096, 3072], P('seq', 'mp')
The draws below stay inside these ranges and needn't reach their ends.
Inputs may be any that keep to these rules, and one draw needn't show every extreme that they name: Pool rows s * 16 .. (s + 1) * 16 - 1 lie on index s of seq; these blocks belong to requests of 16 different indices of seq (block_req // 2); exactly one request, the same on every index, owns one block on every index of seq (16 blocks in all). prefix_blocks[r] is the number of pool blocks b with block_req[b] = r.
All inputs are finite; a program needn't handle non-finite values.
Results may differ from the reference program's by a relative error of at most 0.015.
Values may be sent and summed in bfloat16 or wider, within the bound.
A program may use at most 128 MiB of HBM per device.

```python
import math
import jax
import jax.numpy as jnp
import numpy as np
from jax import lax

HEADS = 24
HD = 128
BLOCK = 128
REQ_DEV = 2
BLK_DEV = 16
TOK_DEV = 256
HW = 3072
TOKENS = 4096
REQUESTS = 32
NBLK = 256
N_SEQ = 16


def query_key_pair(key):
    keys = jax.random.split(jax.random.fold_in(key, 7), 3)
    width = HEADS * HD
    column_scale = 3.0 ** (jnp.arange(width, dtype=jnp.float32) / width)
    queries = jnp.clip(jax.random.normal(keys[1], (TOKENS, width), jnp.float32), -6.0, 6.0) * column_scale
    keys_out = jnp.clip(jax.random.normal(keys[2], (TOKENS, width), jnp.float32), -6.0, 6.0) * column_scale
    return (queries, keys_out)


def draw_q_new(key, part):
    return query_key_pair(key)[0].astype(jnp.bfloat16)


def draw_k_new(key, part):
    return query_key_pair(key)[1].astype(jnp.bfloat16)


def pool_map(key):
    keys = jax.random.split(jax.random.fold_in(key, 11), 5)
    hot = jax.random.randint(keys[0], (), 0, N_SEQ).astype(jnp.int32)
    hot_sub = jax.random.randint(keys[1], (), 0, REQ_DEV).astype(jnp.int32)
    row_keys = jax.random.split(keys[2], N_SEQ)
    perms = jax.vmap(lambda one: jax.random.permutation(one, N_SEQ - 1))(row_keys).astype(jnp.int32)
    others = perms[:, :BLK_DEV - 1]
    others = others + (others >= hot).astype(jnp.int32)
    dests = jnp.concatenate([jnp.zeros((N_SEQ, 1), jnp.int32) + hot, others], 1)
    shift = jax.random.randint(keys[3], (N_SEQ, 1), 0, BLK_DEV).astype(jnp.int32)
    index = (jnp.arange(BLK_DEV, dtype=jnp.int32)[None, :] + shift) % BLK_DEV
    dests = jnp.take_along_axis(dests, index, 1)
    subs = jax.random.randint(keys[4], (N_SEQ, BLK_DEV), 0, REQ_DEV).astype(jnp.int32)
    subs = jnp.where(dests == hot, hot_sub, subs)
    owners = (dests * REQ_DEV + subs).reshape(NBLK).astype(jnp.int32)
    counts = jnp.sum((owners[None, :] == jnp.arange(REQUESTS, dtype=jnp.int32)[:, None]).astype(jnp.int32), 1)
    return (owners, counts.astype(jnp.int32))


def draw_block_req(key, part):
    return pool_map(key)[0]


def draw_prefix_blocks(key, part):
    return pool_map(key)[1]


def draw_cache_k(key, part):
    keys = jax.random.split(jax.random.fold_in(key, 17), 1)
    width = HEADS * HD
    base = jnp.clip(jax.random.normal(keys[0], (NBLK, BLOCK, width), jnp.float32), -6.0, 6.0)
    return base.astype(jnp.bfloat16)


def steps_of(rng, extent, pieces, low, high):
    factor_of, own = 1.0, jax.random.fold_in(rng, 6)
    for dim, parts in pieces:
        heights = jnp.exp(jax.random.uniform(jax.random.fold_in(own, dim), (parts,), jnp.float32, low / len(pieces), high / len(pieces)))
        factor_of = factor_of * jnp.repeat(heights, extent[dim] // parts).reshape([-1 if axis == dim else 1 for axis in range(len(extent))])
    return factor_of


def profile(amount, total, bound, lean):
    loads = [(1 << 20) // math.isqrt(standing ** lean) + 1 for standing in range(2, amount + 1)]
    rest, given = total - bound - (amount - 1), [1] * (amount - 1)
    while rest > 0:
        free = [i for i in range(amount - 1) if given[i] < bound]
        pool, remaining = sum([loads[i] for i in free]), rest
        for i in free:
            addition = min(bound - given[i], max(1, remaining * loads[i] // pool), rest)
            given[i] = given[i] + addition
            rest = rest - addition
    return np.array([bound] + given)


def uneven(rng, count, total, reach, lean):
    if count == 2:
        one = jax.random.randint(rng, (), max(1, total - reach), min(reach, total - 1) + 1)
        return jnp.stack([one, total - one])
    lengths = jnp.asarray(profile(count, total, reach, lean), jnp.int32)
    couples = (count - 1) // 2
    giver, taker = lengths[1:1 + 2 * couples:2], lengths[2:2 + 2 * couples:2]
    slack = jnp.minimum(giver - 1, reach - taker)
    moved = jax.random.randint(jax.random.fold_in(rng, 1), (couples,), 0, 1 << 20) % (slack + 1)
    lengths = lengths.at[1:1 + 2 * couples:2].set(giver - moved).at[2:2 + 2 * couples:2].set(taker + moved)
    return lengths[jax.random.permutation(jax.random.fold_in(rng, 2), count)]


def scatter_about(rng, extent, deviation, limit, shards=(), held_as=jnp.bfloat16):
    drawn = deviation * jax.random.normal(rng, extent, jnp.float32)
    if shards:
        drawn = drawn * steps_of(rng, extent, shards, -0.22, 0.18)
    return jnp.clip(drawn, -limit, limit).astype(held_as)


def setup_inputs(seed: int = 0) -> dict:
    streams_of = jax.random.split(jax.random.key(seed), 11)
    q_new = draw_q_new(jax.random.fold_in(streams_of[10], 71), 0)
    k_new = draw_k_new(jax.random.fold_in(streams_of[10], 71), 0)
    v_new = scatter_about(streams_of[2], (TOKENS, HW), 1.0, 6.0, ((0, 16), (1, 2)))
    q_gain = jnp.clip(1.0 + 0.18 * jax.random.normal(streams_of[3], (HW,), jnp.float32), 0.1, 1.9)
    k_gain = jnp.clip(1.0 + 0.18 * jax.random.normal(streams_of[4], (HW,), jnp.float32), 0.1, 1.9)
    cache_k = draw_cache_k(jax.random.fold_in(streams_of[10], 71), 0)
    cache_v = scatter_about(streams_of[6], (NBLK, BLOCK, HW), 1.0, 6.0, ((0, 16), (2, 2)))
    new_count = jax.vmap(lambda own: uneven(own, REQ_DEV, TOK_DEV, 3 * TOK_DEV // 4, 1))(jax.random.split(streams_of[7], N_SEQ)).reshape((N_SEQ, REQ_DEV)).astype(jnp.int32)
    prefix_blocks = draw_prefix_blocks(jax.random.fold_in(streams_of[10], 71), 0)
    block_req = draw_block_req(jax.random.fold_in(streams_of[10], 71), 0)
    return {"q_new": q_new, "k_new": k_new, "v_new": v_new, "q_gain": q_gain, "k_gain": k_gain, "cache_k": cache_k, "cache_v": cache_v, "new_count": new_count, "prefix_blocks": prefix_blocks, "block_req": block_req}


def rotate(field, position):
    half = field.shape[-1] // 2
    freq = 500000.0 ** (-(jnp.arange(half, dtype=jnp.float32) / half))
    angle = position.astype(jnp.float32)[:, None] * freq[None, :]
    cosine = jnp.cos(angle)[:, None, :]
    sine = jnp.sin(angle)[:, None, :]
    first = field[..., :half]
    second = field[..., half:]
    return jnp.concatenate([first * cosine - second * sine, second * cosine + first * sine], -1)

def token_meta(counts, prefix, first_req, block_len, tokens_here):
    cumul = jnp.cumsum(counts, axis=1)
    starts = cumul - counts
    order = jnp.arange(tokens_here, dtype=jnp.int32)
    local = lax.optimization_barrier(jnp.sum((order[None, :, None] >= cumul[:, None, :]).astype(jnp.int32), -1))
    picker = (local[:, :, None] == jnp.arange(counts.shape[1], dtype=jnp.int32)[None, None, :]).astype(jnp.int32)
    offset = order[None, :] - lax.optimization_barrier(jnp.sum(picker * starts[:, None, :], -1))
    before = lax.optimization_barrier(jnp.sum(picker * prefix[:, None, :], -1))
    return (first_req[:, None] + local, before * block_len + offset)

def norm_rot(field, gain, position):
    values = field.astype(jnp.float32)
    squares = lax.optimization_barrier(jnp.sum(values * values, -1, keepdims=True))
    normed = values * lax.rsqrt(squares / (HEADS * HD) + 1e-06) * gain
    return rotate(normed.reshape(field.shape[0], HEADS, HD), position).astype(jnp.bfloat16)

def reference(q_new, k_new, v_new, q_gain, k_gain, cache_k, cache_v, new_count, prefix_blocks, block_req):
    first_req = jnp.arange(N_SEQ, dtype=jnp.int32) * REQ_DEV
    request, position = token_meta(new_count, prefix_blocks.reshape(N_SEQ, REQ_DEV), first_req, BLOCK, TOK_DEV)
    queries = norm_rot(q_new, q_gain, position.reshape(-1)).reshape(N_SEQ, TOK_DEV, HEADS, HD)
    keys_new = norm_rot(k_new, k_gain, position.reshape(-1)).reshape(N_SEQ, TOK_DEV, HEADS, HD)
    values_new = v_new.reshape(N_SEQ, TOK_DEV, HEADS, HD)
    scale = HD ** (-0.5)
    local_scores = jnp.einsum('nthd,nshd->nhts', queries.astype(jnp.float32), keys_new.astype(jnp.float32)) * scale
    order = jnp.arange(TOK_DEV, dtype=jnp.int32)
    allowed = (request[:, :, None] == request[:, None, :]) & (order[None, :, None] >= order[None, None, :])
    best = lax.optimization_barrier(jnp.max(jnp.where(allowed[:, None], local_scores, -1e+30), -1))

    def block_scores(owner_req, block_k):
        owner = owner_req // REQ_DEV
        here = lax.dynamic_index_in_dim(queries, owner, 0, keepdims=False)
        req_here = lax.dynamic_index_in_dim(request, owner, 0, keepdims=False)
        scores = jnp.einsum('thd,khd->htk', here.astype(jnp.float32), block_k.reshape(BLOCK, HEADS, HD).astype(jnp.float32)) * scale
        return (owner, scores, req_here == owner_req)

    def first_pass(carry, item):
        owner_req, block_k = item
        owner, scores, match = block_scores(owner_req, block_k)
        block_best = jnp.where(match[None, :], lax.optimization_barrier(jnp.max(scores, -1)), -1e+30)
        old = lax.dynamic_index_in_dim(carry, owner, 0, keepdims=False)
        return (lax.dynamic_update_index_in_dim(carry, jnp.maximum(old, block_best), owner, 0), None)
    best, _ = lax.scan(first_pass, best, (block_req, cache_k))
    weights = jnp.where(allowed[:, None], jnp.exp(local_scores - best[..., None]), 0.0)
    total = lax.optimization_barrier(jnp.sum(weights, -1))
    accum = jnp.einsum('nhts,nshd->nhtd', weights.astype(jnp.bfloat16).astype(jnp.float32), values_new.astype(jnp.float32))

    def second_pass(carry, item):
        total_all, accum_all = carry
        owner_req, block_k, block_v = item
        owner, scores, match = block_scores(owner_req, block_k)
        best_here = lax.dynamic_index_in_dim(best, owner, 0, keepdims=False)
        probs = jnp.where(match[None, :, None], jnp.exp(scores - best_here[..., None]), 0.0)
        add_total = lax.optimization_barrier(jnp.sum(probs, -1))
        add_accum = jnp.einsum('htk,khd->htd', probs.astype(jnp.bfloat16).astype(jnp.float32), block_v.reshape(BLOCK, HEADS, HD).astype(jnp.float32))
        old_total = lax.dynamic_index_in_dim(total_all, owner, 0, keepdims=False)
        old_accum = lax.dynamic_index_in_dim(accum_all, owner, 0, keepdims=False)
        total_all = lax.dynamic_update_index_in_dim(total_all, old_total + add_total, owner, 0)
        accum_all = lax.dynamic_update_index_in_dim(accum_all, old_accum + add_accum, owner, 0)
        return ((total_all, accum_all), None)
    (total, accum), _ = lax.scan(second_pass, (total, accum), (block_req, cache_k, cache_v))
    attended = (accum / total[..., None]).astype(jnp.bfloat16)
    return jnp.transpose(attended, (0, 2, 1, 3)).reshape(TOKENS, HEADS * HD)
```

```python
import functools

import jax
import jax.numpy as jnp
from jax import lax
from jax.experimental import pallas as pl
from jax.experimental.pallas import tpu as pltpu
from jax.sharding import PartitionSpec as P

HD = 128
NEGATIVE = -1e30
LOG2E = 1.4426950408889634
MAJOR = 4
VMEM_LIMIT = 62 * 1024 * 1024


def rotate(field, position):
    half = field.shape[-1] // 2
    freq = 500000.0 ** (-(jnp.arange(half, dtype=jnp.float32) / half))
    angle = position.astype(jnp.float32)[:, None] * freq[None, :]
    cosine = jnp.cos(angle)[:, None, :]
    sine = jnp.sin(angle)[:, None, :]
    first = field[..., :half]
    second = field[..., half:]
    return jnp.concatenate([first * cosine - second * sine, second * cosine + first * sine], -1)


def kernel(
    A, B, H, G,
    table, q_ref, k_ref, v_ref, row_req, col_req, ck_hbm, cv_hbm,
    out_ref,
    qall, kc, vc, part, stat, cpart, cstat, xpart, xstat, zpart, zstat, lacc, lstat,
    kv_sem, agz_s, agz_r, agx_s, agx_r, agc_s, agc_r,
    cp_s, cp_r, cs_s, cs_r, xp_s, xp_r, xs_s, xs_r, zp_s, zp_r, zs_s, zs_r,
):
    me = lax.axis_index("seq")
    T = q_ref.shape[1]
    core = lax.rem(me, 2)
    minor = lax.rem(me // 2, B)
    major = me // (2 * B)
    scale = HD ** (-0.5) * LOG2E

    def at(a, b):
        return (lax.rem(major + a + A, A) * B + lax.rem(minor + b + B, B)) * 2 + core

    sibling = me + 1 - 2 * core

    def slot(a, b, c):
        return (a * B + b) * 2 + c

    def remote(src, dst, send, recv, where):
        return pltpu.make_async_remote_copy(
            src_ref=src, dst_ref=dst, send_sem=send, recv_sem=recv,
            device_id={"seq": where}, device_id_type=pl.DeviceIdType.MESH,
        )

    def agz(a):
        return remote(qall.at[0], qall.at[slot(a, 0, 0)], agz_s.at[a], agz_r.at[a], at(-a, 0))

    def agx(a, b):
        i = a * B + b
        return remote(qall.at[slot(a, 0, 0)], qall.at[slot(a, b, 0)], agx_s.at[i], agx_r.at[i], at(0, -b))

    def agc(a, b):
        i = a * B + b
        return remote(qall.at[slot(a, b, 0)], qall.at[slot(a, b, 1)], agc_s.at[i], agc_r.at[i], sibling)

    def rsc(a, b):
        i = a * B + b
        return (
            remote(part.at[slot(a, b, 1)], cpart.at[i], cp_s.at[i], cp_r.at[i], sibling),
            remote(stat.at[slot(a, b, 1)], cstat.at[i], cs_s.at[i], cs_r.at[i], sibling),
        )

    def rsx(a, b):
        i = a * (B - 1) + b - 1
        return (
            remote(part.at[slot(a, b, 0)], xpart.at[i], xp_s.at[i], xp_r.at[i], at(0, b)),
            remote(stat.at[slot(a, b, 0)], xstat.at[i], xs_s.at[i], xs_r.at[i], at(0, b)),
        )

    def rsz(a):
        i = a - 1
        return (
            remote(part.at[slot(a, 0, 0)], zpart.at[i], zp_s.at[i], zp_r.at[i], at(a, 0)),
            remote(stat.at[slot(a, 0, 0)], zstat.at[i], zs_s.at[i], zs_r.at[i], at(a, 0)),
        )

    def start(copies):
        for copy in copies:
            copy.start()

    def arrived(copies):
        for copy in copies:
            copy.wait_recv()

    def sent(copies):
        for copy in copies:
            copy.wait_send()

    def each_b(body):
        if B == 2:
            body(1)
        else:
            lax.fori_loop(1, B, lambda b, _: (body(b), 0)[1], 0)

    copies = [
        pltpu.make_async_copy(ck_hbm, kc, kv_sem.at[0]),
        pltpu.make_async_copy(cv_hbm, vc, kv_sem.at[1]),
    ]
    start(copies)
    qall[0] = q_ref[...]

    barrier = pltpu.get_barrier_semaphore()

    def greet(where):
        pl.semaphore_signal(barrier, inc=1, device_id={"seq": where}, device_id_type=pl.DeviceIdType.MESH)

    greet(sibling)
    for a in range(1, A):
        greet(at(a, 0))
    each_b(lambda b: greet(at(0, b)))
    pl.semaphore_wait(barrier, 1 + (A - 1) + (B - 1))

    def forward(a):
        each_b(lambda b: agx(a, b).start())
        agc(a, 0).start()

    for a in range(1, A):
        agz(a).start()
    forward(0)

    def cols(h):
        return pl.ds(pl.multiple_of(h * HD, HD), HD)

    def heads(body):
        def group(g, _):
            for j in range(G):
                body(g * G + j)
            return 0

        lax.fori_loop(0, H // G, group, 0)

    def local(h):
        s = jnp.dot(k_ref[:, cols(h)], q_ref[cols(h), :], preferred_element_type=jnp.float32)
        order_s = lax.broadcasted_iota(jnp.int32, (T, T), 0)
        order_t = lax.broadcasted_iota(jnp.int32, (T, T), 1)
        allowed = (col_req[...] == row_req[...]) & (order_s <= order_t)
        s = jnp.where(allowed, s, NEGATIVE)
        m = jnp.max(s, 0, keepdims=True)
        p = jnp.exp2((s - m) * scale)
        lstat[pl.ds(h, 1), :] = m
        lstat[pl.ds(H + h, 1), :] = jnp.sum(p, 0, keepdims=True)
        lacc[cols(h), :] = lax.dot_general(
            v_ref[:, cols(h)], p.astype(jnp.bfloat16), (((0,), (0,)), ((), ())),
            preferred_element_type=jnp.float32,
        )

    heads(local)
    for copy in copies:
        copy.wait()

    def compute(i):
        pick = table[0, i]
        token = lax.broadcasted_iota(jnp.int32, (1, T), 1)
        match = (token >= table[1, i]) & (token < table[2, i])

        def one(h):
            k = kc[pick, :, cols(h)]
            v = vc[pick, :, cols(h)]
            s = jnp.dot(k, qall[i, cols(h), :], preferred_element_type=jnp.float32)
            m = jnp.max(s, 0, keepdims=True)
            p = jnp.exp2((s - m) * scale)
            stat[i, pl.ds(h, 1), :] = jnp.where(match, m, NEGATIVE)
            stat[i, pl.ds(H + h, 1), :] = jnp.sum(p, 0, keepdims=True)
            acc = lax.dot_general(
                v, p.astype(jnp.bfloat16), (((0,), (0,)), ((), ())), preferred_element_type=jnp.float32
            )
            part[i, cols(h), :] = acc.astype(jnp.bfloat16)

        heads(one)

    def merge(i, other, ostat, j):
        def one(h):
            m1, m2 = stat[i, pl.ds(h, 1), :], ostat[j, pl.ds(h, 1), :]
            m = jnp.maximum(m1, m2)
            f1, f2 = jnp.exp2((m1 - m) * scale), jnp.exp2((m2 - m) * scale)
            stat[i, pl.ds(h, 1), :] = m
            stat[i, pl.ds(H + h, 1), :] = (
                stat[i, pl.ds(H + h, 1), :] * f1 + ostat[j, pl.ds(H + h, 1), :] * f2
            )
            part[i, cols(h), :] = (
                part[i, cols(h), :].astype(jnp.float32) * f1 + other[j, cols(h), :].astype(jnp.float32) * f2
            ).astype(jnp.bfloat16)

        heads(one)

    def unit(a, b):
        agc(a, b).wait_recv()
        compute(slot(a, b, 1))
        start(rsc(a, b))
        compute(slot(a, b, 0))

    def merge_core(a, b):
        arrived(rsc(a, b))
        merge(slot(a, b, 0), cpart, cstat, a * B + b)

    def merge_minor(a):
        def body(b):
            arrived(rsx(a, b))
            merge(slot(a, 0, 0), xpart, xstat, a * (B - 1) + b - 1)

        each_b(body)

    for a in range(A):
        unit(a, 0)
        if a + 1 < A:
            agz(a + 1).wait_recv()
            forward(a + 1)

        def far(b, a=a):
            agx(a, b).wait_recv()
            agc(a, b).start()
            unit(a, b)

        each_b(far)

        def near(b, a=a):
            merge_core(a, b)
            if a > 0:
                start(rsx(a, b))

        each_b(near)
        merge_core(a, 0)
        if a - 1 >= 1:
            merge_minor(a - 1)
            start(rsz(a - 1))
    each_b(lambda b: start(rsx(0, b)))
    merge_minor(A - 1)
    start(rsz(A - 1))
    merge_minor(0)
    for a in range(1, A):
        arrived(rsz(a))

    def final(h):
        row = pl.ds(h, 1)
        tot = pl.ds(H + h, 1)
        ms = [lstat[row, :], stat[0, row, :]] + [zstat[j, row, :] for j in range(A - 1)]
        m = functools.reduce(jnp.maximum, ms)
        fs = [jnp.exp2((one - m) * scale) for one in ms]
        ls = [lstat[tot, :], stat[0, tot, :]] + [zstat[j, tot, :] for j in range(A - 1)]
        total = sum(f * l for f, l in zip(fs, ls))
        acc = lacc[cols(h), :] * fs[0] + part[0, cols(h), :].astype(jnp.float32) * fs[1]
        for j in range(A - 1):
            acc = acc + zpart[j, cols(h), :].astype(jnp.float32) * fs[2 + j]
        out_ref[:, cols(h)] = jnp.transpose(acc / total).astype(jnp.bfloat16)

    heads(final)

    for a in range(1, A):
        agz(a).wait_send()
        sent(rsz(a))
    for a in range(A):
        agc(a, 0).wait_send()
        sent(rsc(a, 0))

        def done(b, a=a):
            agx(a, b).wait_send()
            agc(a, b).wait_send()
            sent(rsc(a, b))
            sent(rsx(a, b))

        each_b(done)


def visit(queries_t, keys, values, req, cache_k, cache_v, table, n):
    W, T = queries_t.shape
    H = W // HD
    G = next(g for g in (6, 4, 3, 2, 1) if H % g == 0)
    A = MAJOR
    B = n // (2 * A)
    R = -(-2 * H // 8) * 8
    bf, f32 = jnp.bfloat16, jnp.float32
    dma = pltpu.SemaphoreType.DMA
    vm = pl.BlockSpec(memory_space=pltpu.VMEM)
    hbm = pl.BlockSpec(memory_space=pl.ANY)
    blocks = cache_k.shape[0]
    return pl.pallas_call(
        functools.partial(kernel, A, B, H, G),
        out_shape=jax.ShapeDtypeStruct((T, W), bf),
        in_specs=[pl.BlockSpec(memory_space=pltpu.SMEM), vm, vm, vm, vm, vm, hbm, hbm],
        out_specs=vm,
        scratch_shapes=[
            pltpu.VMEM((n, W, T), bf),
            pltpu.VMEM(cache_k.shape, bf),
            pltpu.VMEM(cache_v.shape, bf),
            pltpu.VMEM((n, W, T), bf),
            pltpu.VMEM((n, R, T), f32),
            pltpu.VMEM((A * B, W, T), bf),
            pltpu.VMEM((A * B, R, T), f32),
            pltpu.VMEM((A * (B - 1), W, T), bf),
            pltpu.VMEM((A * (B - 1), R, T), f32),
            pltpu.VMEM((A - 1, W, T), bf),
            pltpu.VMEM((A - 1, R, T), f32),
            pltpu.VMEM((W, T), f32),
            pltpu.VMEM((R, T), f32),
            dma((2,)),
            dma((A,)), dma((A,)),
            dma((A * B,)), dma((A * B,)),
            dma((A * B,)), dma((A * B,)),
            dma((A * B,)), dma((A * B,)), dma((A * B,)), dma((A * B,)),
            dma((A * (B - 1),)), dma((A * (B - 1),)), dma((A * (B - 1),)), dma((A * (B - 1),)),
            dma((A - 1,)), dma((A - 1,)), dma((A - 1,)), dma((A - 1,)),
        ],
        compiler_params=pltpu.CompilerParams(
            collective_id=0, has_side_effects=True, vmem_limit_bytes=VMEM_LIMIT
        ),
        cost_estimate=pl.CostEstimate(
            flops=4 * n * W * T * cache_k.shape[1], bytes_accessed=4 * blocks * cache_k.shape[1] * W,
            transcendentals=n * H * T * cache_k.shape[1],
        ),
    )(table, queries_t, keys, values, req[None, :], req[:, None], cache_k, cache_v)


def shards(
    q_new, k_new, v_new, q_gain, k_gain, cache_k, cache_v, new_count, prefix_blocks, block_req
):
    tokens_here = q_new.shape[0]
    width_all = q_new.shape[1] * lax.axis_size("mp")
    heads_here = q_new.shape[1] // HD
    block_len = cache_k.shape[1]
    blocks_here = cache_k.shape[0]
    slots = lax.axis_size("seq")
    device = lax.axis_index("seq")
    per_dev = new_count.shape[1]
    query_f = q_new.astype(jnp.float32)
    key_f = k_new.astype(jnp.float32)
    square_q, square_k = lax.psum(
        (jnp.sum(query_f * query_f, -1), jnp.sum(key_f * key_f, -1)), "mp"
    )
    index = jnp.arange(per_dev, dtype=jnp.int32)
    ends = jnp.sum(jnp.where(index[:, None] <= index[None, :], new_count[:, :, None], 0), 1)
    starts = ends - new_count
    order = jnp.arange(tokens_here, dtype=jnp.int32)
    my_ends, my_starts = ends[device], starts[device]
    my_prefix = prefix_blocks.reshape(slots, per_dev)[device]
    local = jnp.sum((order[:, None] >= my_ends[None, :]).astype(jnp.int32), -1)
    picker = (local[:, None] == jnp.arange(per_dev, dtype=jnp.int32)[None, :]).astype(jnp.int32)
    position = (
        jnp.sum(picker * my_prefix[None, :], -1) * block_len
        + order - jnp.sum(picker * my_starts[None, :], -1)
    )
    normed_q = query_f * lax.rsqrt(square_q / width_all + 1e-06)[:, None] * q_gain
    normed_k = key_f * lax.rsqrt(square_k / width_all + 1e-06)[:, None] * k_gain
    queries = rotate(normed_q.reshape(tokens_here, heads_here, HD), position).astype(jnp.bfloat16)
    keys = rotate(normed_k.reshape(tokens_here, heads_here, HD), position).astype(jnp.bfloat16)
    queries_t = queries.reshape(tokens_here, heads_here * HD).T
    keys = keys.reshape(tokens_here, heads_here * HD)

    minors = slots // (2 * MAJOR)
    s = jnp.arange(slots, dtype=jnp.int32)
    target = (
        ((device // (2 * minors) + s // (2 * minors)) % MAJOR) * minors
        + (device // 2 + s // 2) % minors
    ) * 2 + (device + s) % 2
    owners = lax.dynamic_slice(block_req, (device * blocks_here,), (blocks_here,))
    hit = (owners // per_dev)[None, :] == target[:, None]
    present = jnp.any(hit, 1)
    pick = jnp.sum(jnp.where(hit, jnp.arange(blocks_here, dtype=jnp.int32)[None, :], 0), 1)
    owner = jnp.sum(jnp.where(hit, owners[None, :], 0), 1)
    begin = jnp.where(present, starts.reshape(-1)[owner], 0)
    finish = jnp.where(present, ends.reshape(-1)[owner], 0)
    table = jnp.stack([pick, begin, finish]).astype(jnp.int32)
    return visit(queries_t, keys, v_new, local, cache_k, cache_v, table, slots)


def solution(mesh):
    return jax.shard_map(
        shards,
        mesh=mesh,
        in_specs=(
            P("seq", "mp"),
            P("seq", "mp"),
            P("seq", "mp"),
            P("mp"),
            P("mp"),
            P("seq", None, "mp"),
            P("seq", None, "mp"),
            P(),
            P(),
            P(),
        ),
        out_specs=P("seq", "mp"),
        check_vma=False,
    )
```

```python
import functools

import jax
import jax.numpy as jnp
from jax import lax
from jax.experimental import pallas as pl
from jax.experimental.pallas import tpu as pltpu
from jax.sharding import PartitionSpec as P

HD = 128
NEGATIVE = -1e30
LOG2E = 1.4426950408889634
MAJOR = 4
VMEM_LIMIT = 62 * 1024 * 1024


def rotate(field, position):
    half = field.shape[-1] // 2
    freq = 500000.0 ** (-(jnp.arange(half, dtype=jnp.float32) / half))
    angle = position.astype(jnp.float32)[:, None] * freq[None, :]
    cosine = jnp.cos(angle)[:, None, :]
    sine = jnp.sin(angle)[:, None, :]
    first = field[..., :half]
    second = field[..., half:]
    return jnp.concatenate([first * cosine - second * sine, second * cosine + first * sine], -1)


def kernel(
    A, B, H, G,
    table, q_ref, k_ref, v_ref, row_req, col_req, ck_hbm, cv_hbm,
    out_ref,
    qall, kc, vc, part, stat, cpart, cstat, xpart, xstat, zpart, zstat, lacc, lstat,
    kv_sem, agz_s, agz_r, agx_s, agx_r, agc_s, agc_r,
    cp_s, cp_r, cs_s, cs_r, xp_s, xp_r, xs_s, xs_r, zp_s, zp_r, zs_s, zs_r,
):
    me = lax.axis_index("seq")
    T = q_ref.shape[1]
    core = lax.rem(me, 2)
    minor = lax.rem(me // 2, B)
    major = me // (2 * B)
    scale = HD ** (-0.5) * LOG2E

    def at(a, b):
        return (lax.rem(major + a + A, A) * B + lax.rem(minor + b + B, B)) * 2 + core

    sibling = me + 1 - 2 * core

    def slot(a, b, c):
        return (a * B + b) * 2 + c

    def remote(src, dst, send, recv, where):
        return pltpu.make_async_remote_copy(
            src_ref=src, dst_ref=dst, send_sem=send, recv_sem=recv,
            device_id={"seq": where}, device_id_type=pl.DeviceIdType.MESH,
        )

    def agz(a):
        return remote(qall.at[0], qall.at[slot(a, 0, 0)], agz_s.at[a], agz_r.at[a], at(-a, 0))

    def agx(a, b):
        i = a * B + b
        return remote(qall.at[slot(a, 0, 0)], qall.at[slot(a, b, 0)], agx_s.at[i], agx_r.at[i], at(0, -b))

    def agc(a, b):
        i = a * B + b
        return remote(qall.at[slot(a, b, 0)], qall.at[slot(a, b, 1)], agc_s.at[i], agc_r.at[i], sibling)

    def rsc(a, b):
        i = a * B + b
        return (
            remote(part.at[slot(a, b, 1)], cpart.at[i], cp_s.at[i], cp_r.at[i], sibling),
            remote(stat.at[slot(a, b, 1)], cstat.at[i], cs_s.at[i], cs_r.at[i], sibling),
        )

    def rsx(a, b):
        i = a * (B - 1) + b - 1
        return (
            remote(part.at[slot(a, b, 0)], xpart.at[i], xp_s.at[i], xp_r.at[i], at(0, b)),
            remote(stat.at[slot(a, b, 0)], xstat.at[i], xs_s.at[i], xs_r.at[i], at(0, b)),
        )

    def rsz(a):
        i = a - 1
        return (
            remote(part.at[slot(a, 0, 0)], zpart.at[i], zp_s.at[i], zp_r.at[i], at(a, 0)),
            remote(stat.at[slot(a, 0, 0)], zstat.at[i], zs_s.at[i], zs_r.at[i], at(a, 0)),
        )

    def start(copies):
        for copy in copies:
            copy.start()

    def arrived(copies):
        for copy in copies:
            copy.wait_recv()

    def sent(copies):
        for copy in copies:
            copy.wait_send()

    def each_b(body):
        if B == 2:
            body(1)
        else:
            lax.fori_loop(1, B, lambda b, _: (body(b), 0)[1], 0)

    copies = [
        pltpu.make_async_copy(ck_hbm, kc, kv_sem.at[0]),
        pltpu.make_async_copy(cv_hbm, vc, kv_sem.at[1]),
    ]
    start(copies)
    qall[0] = q_ref[...]

    barrier = pltpu.get_barrier_semaphore()

    def greet(where):
        pl.semaphore_signal(barrier, inc=1, device_id={"seq": where}, device_id_type=pl.DeviceIdType.MESH)

    greet(sibling)
    for a in range(1, A):
        greet(at(a, 0))
    each_b(lambda b: greet(at(0, b)))
    pl.semaphore_wait(barrier, 1 + (A - 1) + (B - 1))

    def forward(a):
        each_b(lambda b: agx(a, b).start())
        agc(a, 0).start()

    order = [0] + sorted(range(1, A), key=lambda a: (a != A // 2, a))
    agz(order[1]).start()
    forward(0)

    def cols(h):
        return pl.ds(pl.multiple_of(h * HD, HD), HD)

    def heads(body):
        def group(g, _):
            for j in range(G):
                body(g * G + j)
            return 0

        lax.fori_loop(0, H // G, group, 0)

    def local(h):
        s = jnp.dot(k_ref[:, cols(h)], q_ref[cols(h), :], preferred_element_type=jnp.float32)
        order_s = lax.broadcasted_iota(jnp.int32, (T, T), 0)
        order_t = lax.broadcasted_iota(jnp.int32, (T, T), 1)
        allowed = (col_req[...] == row_req[...]) & (order_s <= order_t)
        s = jnp.where(allowed, s, NEGATIVE)
        m = jnp.max(s, 0, keepdims=True)
        p = jnp.exp2((s - m) * scale)
        lstat[pl.ds(h, 1), :] = m
        lstat[pl.ds(H + h, 1), :] = jnp.sum(p, 0, keepdims=True)
        lacc[cols(h), :] = lax.dot_general(
            v_ref[:, cols(h)], p.astype(jnp.bfloat16), (((0,), (0,)), ((), ())),
            preferred_element_type=jnp.float32,
        )

    heads(local)
    for copy in copies:
        copy.wait()

    def compute(i):
        pick = table[0, i]
        token = lax.broadcasted_iota(jnp.int32, (1, T), 1)
        match = (token >= table[1, i]) & (token < table[2, i])

        def one(h):
            k = kc[pick, :, cols(h)]
            v = vc[pick, :, cols(h)]
            s = jnp.dot(k, qall[i, cols(h), :], preferred_element_type=jnp.float32)
            m = jnp.max(s, 0, keepdims=True)
            p = jnp.exp2((s - m) * scale)
            stat[i, pl.ds(h, 1), :] = jnp.where(match, m, NEGATIVE)
            stat[i, pl.ds(H + h, 1), :] = jnp.sum(p, 0, keepdims=True)
            acc = lax.dot_general(
                v, p.astype(jnp.bfloat16), (((0,), (0,)), ((), ())), preferred_element_type=jnp.float32
            )
            part[i, cols(h), :] = acc.astype(jnp.bfloat16)

        heads(one)

    def merge(i, other, ostat, j):
        def one(h):
            m1, m2 = stat[i, pl.ds(h, 1), :], ostat[j, pl.ds(h, 1), :]
            m = jnp.maximum(m1, m2)
            f1, f2 = jnp.exp2((m1 - m) * scale), jnp.exp2((m2 - m) * scale)
            stat[i, pl.ds(h, 1), :] = m
            stat[i, pl.ds(H + h, 1), :] = (
                stat[i, pl.ds(H + h, 1), :] * f1 + ostat[j, pl.ds(H + h, 1), :] * f2
            )
            part[i, cols(h), :] = (
                part[i, cols(h), :].astype(jnp.float32) * f1 + other[j, cols(h), :].astype(jnp.float32) * f2
            ).astype(jnp.bfloat16)

        heads(one)

    def unit(a, b):
        agc(a, b).wait_recv()
        compute(slot(a, b, 1))
        start(rsc(a, b))
        compute(slot(a, b, 0))

    def merge_core(a, b):
        arrived(rsc(a, b))
        merge(slot(a, b, 0), cpart, cstat, a * B + b)

    def merge_minor(a):
        def body(b):
            arrived(rsx(a, b))
            merge(slot(a, 0, 0), xpart, xstat, a * (B - 1) + b - 1)

        each_b(body)

    def pass_on(step):
        if step + 1 < A:
            agz(order[step + 1]).wait_recv()
            forward(order[step + 1])
            agz(order[step + 1]).wait_send()
            if step + 2 < A:
                agz(order[step + 2]).start()

    for step, a in enumerate(order):
        unit(a, 0)
        if step < 2:
            pass_on(step)

        def far(b, a=a):
            agx(a, b).wait_recv()
            agc(a, b).start()
            unit(a, b)

        each_b(far)

        def near(b, a=a):
            merge_core(a, b)
            if a > 0:
                start(rsx(a, b))

        each_b(near)
        if step == A - 1:
            each_b(lambda b: start(rsx(0, b)))
        merge_core(a, 0)
        if step >= 2:
            pass_on(step)
            merge_minor(order[step - 1])
            start(rsz(order[step - 1]))
    merge_minor(order[-1])
    start(rsz(order[-1]))
    merge_minor(0)
    for a in range(1, A):
        arrived(rsz(a))

    def final(h):
        row = pl.ds(h, 1)
        tot = pl.ds(H + h, 1)
        ms = [lstat[row, :], stat[0, row, :]] + [zstat[j, row, :] for j in range(A - 1)]
        m = functools.reduce(jnp.maximum, ms)
        fs = [jnp.exp2((one - m) * scale) for one in ms]
        ls = [lstat[tot, :], stat[0, tot, :]] + [zstat[j, tot, :] for j in range(A - 1)]
        total = sum(f * l for f, l in zip(fs, ls))
        acc = lacc[cols(h), :] * fs[0] + part[0, cols(h), :].astype(jnp.float32) * fs[1]
        for j in range(A - 1):
            acc = acc + zpart[j, cols(h), :].astype(jnp.float32) * fs[2 + j]
        out_ref[:, cols(h)] = jnp.transpose(acc / total).astype(jnp.bfloat16)

    heads(final)

    for a in range(1, A):
        sent(rsz(a))
    for a in range(A):
        agc(a, 0).wait_send()
        sent(rsc(a, 0))

        def done(b, a=a):
            agx(a, b).wait_send()
            agc(a, b).wait_send()
            sent(rsc(a, b))
            sent(rsx(a, b))

        each_b(done)


def visit(queries_t, keys, values, req, cache_k, cache_v, table, n):
    W, T = queries_t.shape
    H = W // HD
    G = next(g for g in (6, 4, 3, 2, 1) if H % g == 0)
    A = MAJOR
    B = n // (2 * A)
    R = -(-2 * H // 8) * 8
    bf, f32 = jnp.bfloat16, jnp.float32
    dma = pltpu.SemaphoreType.DMA
    vm = pl.BlockSpec(memory_space=pltpu.VMEM)
    hbm = pl.BlockSpec(memory_space=pl.ANY)
    blocks = cache_k.shape[0]
    return pl.pallas_call(
        functools.partial(kernel, A, B, H, G),
        out_shape=jax.ShapeDtypeStruct((T, W), bf),
        in_specs=[pl.BlockSpec(memory_space=pltpu.SMEM), vm, vm, vm, vm, vm, hbm, hbm],
        out_specs=vm,
        scratch_shapes=[
            pltpu.VMEM((n, W, T), bf),
            pltpu.VMEM(cache_k.shape, bf),
            pltpu.VMEM(cache_v.shape, bf),
            pltpu.VMEM((n, W, T), bf),
            pltpu.VMEM((n, R, T), f32),
            pltpu.VMEM((A * B, W, T), bf),
            pltpu.VMEM((A * B, R, T), f32),
            pltpu.VMEM((A * (B - 1), W, T), bf),
            pltpu.VMEM((A * (B - 1), R, T), f32),
            pltpu.VMEM((A - 1, W, T), bf),
            pltpu.VMEM((A - 1, R, T), f32),
            pltpu.VMEM((W, T), f32),
            pltpu.VMEM((R, T), f32),
            dma((2,)),
            dma((A,)), dma((A,)),
            dma((A * B,)), dma((A * B,)),
            dma((A * B,)), dma((A * B,)),
            dma((A * B,)), dma((A * B,)), dma((A * B,)), dma((A * B,)),
            dma((A * (B - 1),)), dma((A * (B - 1),)), dma((A * (B - 1),)), dma((A * (B - 1),)),
            dma((A - 1,)), dma((A - 1,)), dma((A - 1,)), dma((A - 1,)),
        ],
        compiler_params=pltpu.CompilerParams(
            collective_id=0, has_side_effects=True, vmem_limit_bytes=VMEM_LIMIT
        ),
        cost_estimate=pl.CostEstimate(
            flops=4 * n * W * T * cache_k.shape[1], bytes_accessed=4 * blocks * cache_k.shape[1] * W,
            transcendentals=n * H * T * cache_k.shape[1],
        ),
    )(table, queries_t, keys, values, req[None, :], req[:, None], cache_k, cache_v)


def shards(
    q_new, k_new, v_new, q_gain, k_gain, cache_k, cache_v, new_count, prefix_blocks, block_req
):
    tokens_here = q_new.shape[0]
    width_all = q_new.shape[1] * lax.axis_size("mp")
    heads_here = q_new.shape[1] // HD
    block_len = cache_k.shape[1]
    blocks_here = cache_k.shape[0]
    slots = lax.axis_size("seq")
    device = lax.axis_index("seq")
    per_dev = new_count.shape[1]
    query_f = q_new.astype(jnp.float32)
    key_f = k_new.astype(jnp.float32)
    square_q, square_k = lax.psum(
        (jnp.sum(query_f * query_f, -1), jnp.sum(key_f * key_f, -1)), "mp"
    )
    index = jnp.arange(per_dev, dtype=jnp.int32)
    ends = jnp.sum(jnp.where(index[:, None] <= index[None, :], new_count[:, :, None], 0), 1)
    starts = ends - new_count
    order = jnp.arange(tokens_here, dtype=jnp.int32)
    my_ends, my_starts = ends[device], starts[device]
    my_prefix = prefix_blocks.reshape(slots, per_dev)[device]
    local = jnp.sum((order[:, None] >= my_ends[None, :]).astype(jnp.int32), -1)
    picker = (local[:, None] == jnp.arange(per_dev, dtype=jnp.int32)[None, :]).astype(jnp.int32)
    position = (
        jnp.sum(picker * my_prefix[None, :], -1) * block_len
        + order - jnp.sum(picker * my_starts[None, :], -1)
    )
    normed_q = query_f * lax.rsqrt(square_q / width_all + 1e-06)[:, None] * q_gain
    normed_k = key_f * lax.rsqrt(square_k / width_all + 1e-06)[:, None] * k_gain
    queries = rotate(normed_q.reshape(tokens_here, heads_here, HD), position).astype(jnp.bfloat16)
    keys = rotate(normed_k.reshape(tokens_here, heads_here, HD), position).astype(jnp.bfloat16)
    queries_t = queries.reshape(tokens_here, heads_here * HD).T
    keys = keys.reshape(tokens_here, heads_here * HD)

    minors = slots // (2 * MAJOR)
    s = jnp.arange(slots, dtype=jnp.int32)
    target = (
        ((device // (2 * minors) + s // (2 * minors)) % MAJOR) * minors
        + (device // 2 + s // 2) % minors
    ) * 2 + (device + s) % 2
    owners = lax.dynamic_slice(block_req, (device * blocks_here,), (blocks_here,))
    hit = (owners // per_dev)[None, :] == target[:, None]
    present = jnp.any(hit, 1)
    pick = jnp.sum(jnp.where(hit, jnp.arange(blocks_here, dtype=jnp.int32)[None, :], 0), 1)
    owner = jnp.sum(jnp.where(hit, owners[None, :], 0), 1)
    begin = jnp.where(present, starts.reshape(-1)[owner], 0)
    finish = jnp.where(present, ends.reshape(-1)[owner], 0)
    table = jnp.stack([pick, begin, finish]).astype(jnp.int32)
    return visit(queries_t, keys, v_new, local, cache_k, cache_v, table, slots)


def solution(mesh):
    return jax.shard_map(
        shards,
        mesh=mesh,
        in_specs=(
            P("seq", "mp"),
            P("seq", "mp"),
            P("seq", "mp"),
            P("mp"),
            P("mp"),
            P("seq", None, "mp"),
            P("seq", None, "mp"),
            P(),
            P(),
            P(),
        ),
        out_specs=P("seq", "mp"),
        check_vma=False,
    )
```
